32 devices in a mesh: dp: 4 (over z), mp: 8 (over y, x, core).
Axes of the slice: x: 2, y: 2, z: 4, core: 2. Of those that a mesh axis runs over, the one named last changes fastest.
Arguments:
- tokens: bfloat16 [8192, 16384], P('dp', 'mp'), may hold values from -6 to 6
- inner_one: bfloat16 [128, 128, 128], P('mp'), may hold values from -0.5 to 0.5
- outer_one: bfloat16 [128, 128, 128], P('mp'), may hold values from -0.5 to 0.5
- inner_two: bfloat16 [128, 128, 128], P('mp'), may hold values from -0.5 to 0.5
- outer_two: bfloat16 [128, 128, 128], P('mp'), may hold values from -0.5 to 0.5
- cotangent: bfloat16 [8192, 16384], P('dp', 'mp'), may hold values from -6 to 6
Outputs:
- output: bfloat16 [8192, 16384], P('dp', 'mp')
- input_grad: bfloat16 [8192, 16384], P('dp', 'mp')
- inner_one_grad: float32 [128, 128, 128], P('mp', 'dp')
- outer_one_grad: float32 [128, 128, 128], P('mp', 'dp')
- inner_two_grad: float32 [128, 128, 128], P('mp', 'dp')
- outer_two_grad: float32 [128, 128, 128], P('mp', 'dp')
The draws below stay inside these ranges and needn't reach their ends.
All inputs are finite; a program needn't handle non-finite values.
Results may differ from the reference program's by a relative error of at most 0.0069.
Values may be sent and summed in bfloat16 or wider, within the bound.
A program may use at most 192 MiB of HBM per device.

```python
from functools import partial
import jax
import jax.numpy as jnp
from jax import lax

NB = 128
TOK_DEV = 2048
D = 16384
TOKENS = 8192
N_DP = 4


def block_scale(stream_key, extent, cuts, least, top_value):
    gain = 1.0
    for axis_at, shards_of in cuts:
        heights = jax.random.uniform(jax.random.fold_in(jax.random.fold_in(stream_key, 6), axis_at), (shards_of,), jnp.float32, least / len(cuts), top_value / len(cuts))
        gain = gain * jnp.repeat(jnp.exp(heights), extent[axis_at] // shards_of).reshape((-1,) + (1,) * (len(extent) - 1 - axis_at))
    return gain


def noise(key, shape, scale, bound, cuts=(), kind=jnp.bfloat16):
    array = scale * jax.random.normal(key, shape, jnp.float32)
    if cuts:
        array = array * block_scale(key, shape, cuts, -0.22, 0.18)
    return jnp.clip(array, -bound, bound).astype(kind)


def setup_inputs(seed: int = 0) -> dict:
    key_of = jax.random.split(jax.random.key(seed), 7)
    return {
        "tokens": noise(key_of[0], (TOKENS, D), 1.0, 6.0, ((0, 4), (1, 8))),
        "inner_one": noise(key_of[1], (NB, NB, NB), NB ** -0.5, 0.5, ((0, 8),)),
        "outer_one": noise(key_of[2], (NB, NB, NB), NB ** -0.5, 0.5, ((0, 8),)),
        "inner_two": noise(key_of[3], (NB, NB, NB), NB ** -0.5, 0.5, ((0, 8),)),
        "outer_two": noise(key_of[4], (NB, NB, NB), NB ** -0.5, 0.5, ((0, 8),)),
        "cotangent": noise(key_of[5], (TOKENS, D), 1.0, 6.0, ((0, 4), (1, 8))),
    }


def gelu_tanh(values):
    return jax.nn.gelu(values, approximate=True)

def rounded(values):
    return lax.optimization_barrier(values.astype(jnp.bfloat16))

def as_float(values):
    return values.astype(jnp.float32)

def one_block(weights, totals, pieces):
    x_block, g_block = pieces
    tok_rows = x_block.shape[0]
    inputs = x_block.reshape(tok_rows, NB, NB)
    grads = g_block.reshape(tok_rows, NB, NB)
    w_one, o_one, w_two, o_two = weights
    first_mid = rounded(jnp.einsum('tbk,bkj->tbj', as_float(inputs), as_float(w_one)))
    first_perm = jnp.transpose(first_mid, (0, 2, 1))
    pre_act = jnp.einsum('tjb,jbl->tjl', as_float(first_perm), as_float(o_one))
    hidden = rounded(gelu_tanh(pre_act))
    second_mid = rounded(jnp.einsum('tbk,bkj->tbj', as_float(hidden), as_float(w_two)))
    second_perm = jnp.transpose(second_mid, (0, 2, 1))
    output = jnp.einsum('tjb,jbl->tjl', as_float(second_perm), as_float(o_two)).astype(jnp.bfloat16)
    grad_perm_two = rounded(jnp.einsum('tjl,jbl->tjb', as_float(grads), as_float(o_two)))
    grad_mid_two = jnp.transpose(grad_perm_two, (0, 2, 1))
    grad_hidden = jnp.einsum('tbj,bkj->tbk', as_float(grad_mid_two), as_float(w_two))
    primal_out, pullback = jax.vjp(gelu_tanh, pre_act)
    grad_pre = rounded(pullback(grad_hidden)[0])
    grad_perm_one = rounded(jnp.einsum('tjl,jbl->tjb', as_float(grad_pre), as_float(o_one)))
    grad_mid_one = jnp.transpose(grad_perm_one, (0, 2, 1))
    input_grad = jnp.einsum('tbj,bkj->tbk', as_float(grad_mid_one), as_float(w_one)).astype(jnp.bfloat16)
    outer_two_grad = jnp.einsum('tjb,tjl->jbl', as_float(second_perm), as_float(grads))
    inner_two_grad = jnp.einsum('tbk,tbj->bkj', as_float(hidden), as_float(grad_mid_two))
    outer_one_grad = jnp.einsum('tjb,tjl->jbl', as_float(first_perm), as_float(grad_pre))
    inner_one_grad = jnp.einsum('tbk,tbj->bkj', as_float(inputs), as_float(grad_mid_one))
    new_totals = (totals[0] + inner_one_grad, totals[1] + outer_one_grad, totals[2] + inner_two_grad, totals[3] + outer_two_grad)
    return (new_totals, (output.reshape(tok_rows, D), input_grad.reshape(tok_rows, D)))

def reference(tokens, inner_one, outer_one, inner_two, outer_two, cotangent):
    weights = (inner_one, outer_one, inner_two, outer_two)
    empty = jnp.zeros((NB, NB, NB), jnp.float32)
    starts = (empty, empty, empty, empty)
    stacked = (tokens.reshape(N_DP, TOK_DEV, D), cotangent.reshape(N_DP, TOK_DEV, D))
    totals, results = lax.scan(partial(one_block, weights), starts, stacked)
    output = results[0].reshape(TOKENS, D)
    input_grad = results[1].reshape(TOKENS, D)
    return (output, input_grad, totals[0], totals[1], totals[2], totals[3])
```

```python
import jax
import jax.numpy as jnp
from jax import lax
from jax.sharding import PartitionSpec as P

PARTS = 2


def gelu_tanh(values):
    return jax.nn.gelu(values, approximate=True)


def product(form, left, right):
    return jnp.einsum(form, left, right, preferred_element_type=jnp.float32)


def forward(values):
    return lax.all_to_all(values, "mp", split_axis=0, concat_axis=1, tiled=True)


def back(values):
    return lax.all_to_all(values, "mp", split_axis=1, concat_axis=0, tiled=True)


def after(value, earlier):
    return lax.optimization_barrier((value, earlier))[0]


def body(tokens, inner_one, outer_one, inner_two, outer_two, cotangent):
    tok_rows = tokens.shape[0]
    local_blocks = inner_one.shape[0]
    block_size = inner_one.shape[1]
    rows = tok_rows // PARTS
    inputs, grads, first_perm, grad_mid_two = [], [], [], []
    arrived = None
    for part in range(PARTS):
        cut = slice(part * rows, (part + 1) * rows)
        x_part = tokens[cut].reshape(rows, local_blocks, block_size)
        g_part = cotangent[cut].reshape(rows, local_blocks, block_size)
        inputs.append(x_part)
        grads.append(g_part)
        first_mid = product("tbk,bkj->jbt", x_part, inner_one).astype(jnp.bfloat16)
        if arrived is None:
            g_part = after(g_part, first_mid)
        else:
            first_mid = after(first_mid, arrived)
        arrived = forward(first_mid)
        first_perm.append(arrived)
        grad_perm_two = product("tjl,jbl->jbt", g_part, outer_two).astype(jnp.bfloat16)
        arrived = back(after(grad_perm_two, arrived))
        grad_mid_two.append(arrived)
    second_perm, grad_mid_one = [], []
    inner_two_grad = outer_one_grad = outer_two_grad = inner_one_grad = 0.0
    output, input_grad = [], []
    for part in range(PARTS):
        pre_act = product("jbt,jbl->tjl", first_perm[part], outer_one)
        hidden = gelu_tanh(pre_act).astype(jnp.bfloat16)
        second_mid = product("tbk,bkj->jbt", hidden, inner_two).astype(jnp.bfloat16)
        arrived = forward(after(second_mid, arrived))
        second_perm.append(arrived)
        grad_hidden = product("jbt,bkj->tbk", grad_mid_two[part], inner_two)
        inner_two_grad += product("tbk,jbt->bkj", hidden, grad_mid_two[part])
        primal_out, pullback = jax.vjp(gelu_tanh, pre_act)
        grad_pre = pullback(grad_hidden)[0].astype(jnp.bfloat16)
        grad_perm_one = product("tjl,jbl->jbt", grad_pre, outer_one).astype(jnp.bfloat16)
        arrived = back(after(grad_perm_one, arrived))
        grad_mid_one.append(arrived)
        outer_one_grad += product("jbt,tjl->jbl", first_perm[part], grad_pre)
    for part in range(PARTS):
        output.append(product("jbt,jbl->tjl", second_perm[part], outer_two).astype(jnp.bfloat16))
        outer_two_grad += product("jbt,tjl->jbl", second_perm[part], grads[part])
        inner_one_grad += product("tbk,jbt->bkj", inputs[part], grad_mid_one[part])
        input_grad.append(product("jbt,bkj->tbk", grad_mid_one[part], inner_one).astype(jnp.bfloat16))

    def total(grad):
        return lax.psum_scatter(grad, "dp", scatter_dimension=1, tiled=True)

    width_here = local_blocks * block_size
    return (
        jnp.concatenate(output).reshape(tok_rows, width_here),
        jnp.concatenate(input_grad).reshape(tok_rows, width_here),
        total(inner_one_grad),
        total(outer_one_grad),
        total(inner_two_grad),
        total(outer_two_grad),
    )


def solution(mesh):
    placed = (
        P("dp", "mp"),
        P("mp", None, None),
        P("mp", None, None),
        P("mp", None, None),
        P("mp", None, None),
        P("dp", "mp"),
    )
    return jax.shard_map(
        body,
        mesh=mesh,
        in_specs=placed,
        out_specs=(
            P("dp", "mp"),
            P("dp", "mp"),
            P("mp", "dp", None),
            P("mp", "dp", None),
            P("mp", "dp", None),
            P("mp", "dp", None),
        ),
        check_vma=False,
    )
```

```python
import functools
import jax
import jax.numpy as jnp
from jax import lax
from jax.experimental import pallas as pl
from jax.experimental.pallas import tpu as pltpu
from jax.sharding import PartitionSpec as P

MESH = pl.DeviceIdType.MESH
CHUNK = 256
LANES = 128
SLOTS = 2
LAG_MIDDLE = 2
LAG_LAST = 4
ROOT_2_PI = 0.7978845608028654
CUBIC = 0.044715


def dot(left, right, left_axis, right_axis):
    return lax.dot_general(
        left, right, (((left_axis,), (right_axis,)), ((), ())),
        preferred_element_type=jnp.float32,
    )


def monarch_kernel(
    peers, chunks, blocks, size,
    x_hbm, g_hbm, w1t, o1, o1t, w2, w2t, o2,
    out_hbm, ig_hbm, i1_grad, o1_grad, i2_grad, o2_grad,
    recv, send, stage, tiles_in, tiles_out,
    send_sem, recv_sem, own_sem, in_sem, out_sem,
):
    dp, me = lax.axis_index("dp"), lax.axis_index("mp")
    halves = CHUNK // LANES
    copies, stores = {}, {}

    barrier = pltpu.get_barrier_semaphore()
    for step in range(1, peers):
        pl.semaphore_signal(
            barrier, inc=1, device_id=(dp, lax.rem(me + step, peers)), device_id_type=MESH
        )

    def load(which, source, chunk):
        copy = pltpu.make_async_copy(
            source.at[pl.ds(chunk * CHUNK, CHUNK)], tiles_in.at[which], in_sem.at[which]
        )
        copy.start()
        copies["in", which] = copy

    def store(which, target, chunk):
        copy = pltpu.make_async_copy(
            tiles_out.at[which], target.at[pl.ds(chunk * CHUNK, CHUNK)], out_sem.at[which]
        )
        copy.start()
        stores[which] = copy

    def columns(block):
        return pl.ds(pl.multiple_of(block * size, size), size)

    def spread(which, block, values):
        for half in range(halves):
            stage[which, half, pl.ds(block, size, stride=blocks), :] = values[
                :, half * LANES : (half + 1) * LANES
            ]

    def release(kind, chunk):
        for copy in copies.pop(("send", kind, chunk), ()):
            copy.wait_send()

    def dispatch(kind, chunk, which):
        release(kind, chunk - SLOTS)
        held = send.at[kind, chunk % SLOTS]
        if chunk >= SLOTS:
            copies.pop(("own", kind, chunk - SLOTS)).wait()

        @pl.loop(0, size, unroll=8)
        def _(row):
            for half in range(halves):
                held[row, :, half * LANES : (half + 1) * LANES] = stage[
                    which, half, pl.ds(pl.multiple_of(row * blocks, blocks), blocks), :
                ].astype(jnp.bfloat16)

        def rows(peer):
            return pl.ds(pl.multiple_of(peer * blocks, blocks), blocks)

        place = recv.at[kind, chunk, :, rows(me), :]
        started = []
        for step in range(1, peers):
            peer = lax.rem(me + step, peers)
            copy = pltpu.make_async_remote_copy(
                src_ref=held.at[rows(peer)],
                dst_ref=place,
                send_sem=send_sem.at[kind, chunk % SLOTS, step],
                recv_sem=recv_sem.at[kind, chunk, step],
                device_id=(dp, peer),
                device_id_type=MESH,
            )
            copy.start()
            started.append(copy)
        copies["send", kind, chunk] = started
        copies["recv", kind, chunk] = started
        own = pltpu.make_async_copy(held.at[rows(me)], place, own_sem.at[kind, chunk % SLOTS])
        own.start()
        copies["own", kind, chunk] = own

    def arrive(kind, chunk):
        for copy in copies.pop(("recv", kind, chunk)):
            copy.wait_recv()
        own = copies.pop(("own", kind, chunk), None)
        if own is not None:
            own.wait()
            copies["own", kind, chunk] = DONE

    def first(chunk):
        for kind, weight, source in ((0, w1t, x_hbm), (1, o2, g_hbm)):
            copies["in", kind].wait()

            @pl.loop(0, blocks, unroll=4)
            def _(block):
                spread(kind, block, dot(weight[block], tiles_in[kind, :, columns(block)], 1, 1))

            if chunk + 1 < chunks:
                load(kind, source, chunk + 1)
            if kind == 0 and chunk == 0:
                pl.semaphore_wait(barrier, peers - 1)
            dispatch(kind, chunk, kind)

    def middle(chunk):
        arrive(0, chunk)
        arrive(1, chunk)

        @pl.loop(0, blocks, unroll=2)
        def _(block):
            perm = recv[0, chunk, block]
            value = dot(o1t[block], perm, 1, 0)
            square = value * value
            bent = jnp.tanh(ROOT_2_PI * value * (1.0 + CUBIC * square))
            rise = 0.5 + 0.5 * bent
            slope = rise + (0.5 * ROOT_2_PI) * value * (1.0 - bent * bent) * (
                1.0 + (3.0 * CUBIC) * square
            )
            hidden = (value * rise).astype(jnp.bfloat16)
            back = recv[1, chunk, block]
            grad_pre = (dot(w2[block], back, 1, 0) * slope).astype(jnp.bfloat16)
            spread(0, block, dot(w2t[block], hidden, 1, 0))
            spread(1, block, dot(o1[block], grad_pre, 1, 0))
            i2_grad[block] += dot(hidden, back, 1, 1)
            o1_grad[block] += dot(perm, grad_pre, 1, 1)

        dispatch(2, chunk, 0)
        dispatch(3, chunk, 1)

    def last(chunk):
        for kind, weight, total, source, target in (
            (2, o2, o2_grad, g_hbm, out_hbm), (3, w1t, i1_grad, x_hbm, ig_hbm)
        ):
            arrive(kind, chunk)
            copies["in", kind].wait()
            if chunk:
                stores[kind - 2].wait()

            @pl.loop(0, blocks, unroll=4)
            def _(block):
                part = recv[kind, chunk, block]
                tiles_out[kind - 2, :, columns(block)] = dot(
                    part, weight[block], 0, 0
                ).astype(jnp.bfloat16)
                total[block] += dot(part, tiles_in[kind, :, columns(block)], 1, 0)

            store(kind - 2, target, chunk)
            if chunk + 1 < chunks:
                load(kind, source, chunk + 1)

    for which, source in enumerate((x_hbm, g_hbm, g_hbm, x_hbm)):
        load(which, source, 0)
    for total in (i1_grad, o1_grad, i2_grad, o2_grad):
        total[...] = jnp.zeros_like(total)
    for step in range(chunks + LAG_LAST):
        if step < chunks:
            first(step)
        if 0 <= step - LAG_MIDDLE < chunks:
            middle(step - LAG_MIDDLE)
        if 0 <= step - LAG_LAST < chunks:
            last(step - LAG_LAST)
    for kind in range(4):
        for chunk in range(chunks):
            release(kind, chunk)
    for copy in stores.values():
        copy.wait()

    @pl.loop(0, blocks)
    def _(block):
        i1_grad[block] = i1_grad[block].T


class Done:
    def wait(self):
        pass


DONE = Done()


def fused(peers, tokens, inner_one, outer_one, inner_two, outer_two, cotangent):
    tok_rows, width = tokens.shape
    blocks, size, _ = inner_one.shape
    chunks = tok_rows // CHUNK
    in_vmem = pl.BlockSpec(memory_space=pltpu.VMEM)
    anywhere = pl.BlockSpec(memory_space=pl.ANY)
    grad = jax.ShapeDtypeStruct((blocks, size, size), jnp.float32)
    wide = jax.ShapeDtypeStruct((tok_rows, width), jnp.bfloat16)
    turned = lambda weight: jnp.swapaxes(weight, 1, 2)
    results = pl.pallas_call(
        functools.partial(monarch_kernel, peers, chunks, blocks, size),
        out_shape=(wide, wide, grad, grad, grad, grad),
        in_specs=[anywhere] * 2 + [in_vmem] * 6,
        out_specs=(anywhere,) * 2 + (in_vmem,) * 4,
        scratch_shapes=[
            pltpu.VMEM((4, chunks, blocks, size, CHUNK), jnp.bfloat16),
            pltpu.VMEM((4, SLOTS, size, blocks, CHUNK), jnp.bfloat16),
            pltpu.VMEM((2, CHUNK // LANES, size * blocks, LANES), jnp.float32),
            pltpu.VMEM((4, CHUNK, width), jnp.bfloat16),
            pltpu.VMEM((2, CHUNK, width), jnp.bfloat16),
            pltpu.SemaphoreType.DMA((4, SLOTS, peers)),
            pltpu.SemaphoreType.DMA((4, chunks, peers)),
            pltpu.SemaphoreType.DMA((4, SLOTS)),
            pltpu.SemaphoreType.DMA((4,)),
            pltpu.SemaphoreType.DMA((2,)),
        ],
        compiler_params=pltpu.CompilerParams(
            collective_id=0, has_side_effects=True, vmem_limit_bytes=62 * 1024 * 1024
        ),
        cost_estimate=pl.CostEstimate(
            flops=24 * tok_rows * width * size, bytes_accessed=12 * tok_rows * width,
            transcendentals=tok_rows * width,
        ),
    )(
        tokens, cotangent, turned(inner_one), outer_one, turned(outer_one),
        inner_two, turned(inner_two), outer_two,
    )
    sums = [
        lax.psum_scatter(total, "dp", scatter_dimension=1, tiled=True) for total in results[2:]
    ]
    return (*results[:2], *sums)


def gelu_tanh(values):
    return jax.nn.gelu(values, approximate=True)


def product(form, left, right):
    return jnp.einsum(form, left, right, preferred_element_type=jnp.float32)


def return_second(grads, outer_two):
    grad_perm_two = product("tjl,jbl->jbt", grads, outer_two).astype(jnp.bfloat16)
    return lax.all_to_all(grad_perm_two, "mp", split_axis=1, concat_axis=0, tiled=True)


def body(tokens, inner_one, outer_one, inner_two, outer_two, cotangent):
    tok_rows = tokens.shape[0]
    local_blocks = inner_one.shape[0]
    block_size = inner_one.shape[1]
    if local_blocks == 16 and block_size == LANES and tok_rows % CHUNK == 0:
        return fused(
            lax.axis_size("mp"), tokens, inner_one, outer_one, inner_two, outer_two, cotangent
        )
    inputs = tokens.reshape(tok_rows, local_blocks, block_size)
    grads = cotangent.reshape(tok_rows, local_blocks, block_size)
    first_mid = product("tbk,bkj->jbt", inputs, inner_one).astype(jnp.bfloat16)
    first_perm = lax.all_to_all(first_mid, "mp", split_axis=0, concat_axis=1, tiled=True)
    pre_act = product("jbt,jbl->tjl", first_perm, outer_one)
    hidden = gelu_tanh(pre_act).astype(jnp.bfloat16)
    second_mid = product("tbk,bkj->jbt", hidden, inner_two).astype(jnp.bfloat16)
    second_perm = lax.all_to_all(second_mid, "mp", split_axis=0, concat_axis=1, tiled=True)
    output = product("jbt,jbl->tjl", second_perm, outer_two).astype(jnp.bfloat16)
    outer_two_grad = product("jbt,tjl->jbl", second_perm, grads)
    outer_two_grad = lax.psum_scatter(outer_two_grad, "dp", scatter_dimension=1, tiled=True)
    grad_mid_two = return_second(grads, outer_two)
    grad_hidden = product("jbt,bkj->tbk", grad_mid_two, inner_two)
    inner_two_grad = product("tbk,jbt->bkj", hidden, grad_mid_two)
    inner_two_grad = lax.psum_scatter(inner_two_grad, "dp", scatter_dimension=1, tiled=True)
    primal_out, pullback = jax.vjp(gelu_tanh, pre_act)
    grad_pre = pullback(grad_hidden)[0].astype(jnp.bfloat16)
    grad_perm_one = product("tjl,jbl->jbt", grad_pre, outer_one).astype(jnp.bfloat16)
    outer_one_grad = product("jbt,tjl->jbl", first_perm, grad_pre)
    outer_one_grad = lax.psum_scatter(outer_one_grad, "dp", scatter_dimension=1, tiled=True)
    grad_mid_one = lax.all_to_all(grad_perm_one, "mp", split_axis=1, concat_axis=0, tiled=True)
    input_grad = product("jbt,bkj->tbk", grad_mid_one, inner_one).astype(jnp.bfloat16)
    inner_one_grad = product("tbk,jbt->bkj", inputs, grad_mid_one)
    inner_one_grad = lax.psum_scatter(inner_one_grad, "dp", scatter_dimension=1, tiled=True)
    width_here = local_blocks * block_size
    return (
        output.reshape(tok_rows, width_here),
        input_grad.reshape(tok_rows, width_here),
        inner_one_grad,
        outer_one_grad,
        inner_two_grad,
        outer_two_grad,
    )


def solution(mesh):
    placed = (
        P("dp", "mp"),
        P("mp", None, None),
        P("mp", None, None),
        P("mp", None, None),
        P("mp", None, None),
        P("dp", "mp"),
    )
    return jax.shard_map(
        body,
        mesh=mesh,
        in_specs=placed,
        out_specs=(
            P("dp", "mp"),
            P("dp", "mp"),
            P("mp", "dp", None),
            P("mp", "dp", None),
            P("mp", "dp", None),
            P("mp", "dp", None),
        ),
        check_vma=False,
    )
```

```python
import functools
import jax
import jax.numpy as jnp
from jax import lax
from jax.experimental import pallas as pl
from jax.experimental.pallas import tpu as pltpu
from jax.sharding import PartitionSpec as P

MESH = pl.DeviceIdType.MESH
CHUNK = 256
LANES = 128
SLOTS = 2
LAG_MIDDLE = 2
LAG_LAST = 4
SPARE = 16
ROOT_2_PI = 0.7978845608028654
CUBIC = 0.044715


def dot(left, right, left_axis, right_axis):
    return lax.dot_general(
        left, right, (((left_axis,), (right_axis,)), ((), ())),
        preferred_element_type=jnp.float32,
    )


def monarch_kernel(
    peers, replicas, chunks, blocks, size,
    x_hbm, g_hbm, w1, o1, w2, o2,
    out_hbm, ig_hbm, i1_grad, o1_sum, i2_sum, o2_sum,
    recv, send, stage, tiles_in, tiles_out,
    w1t, o1t, w2t, o1_grad, i2_grad, o2_grad, shares, landing,
    send_sem, recv_sem, own_sem, in_sem, out_sem, share_sem, landing_sem,
):
    dp, me = lax.axis_index("dp"), lax.axis_index("mp")
    halves = CHUNK // LANES
    slab = size // replicas
    copies, stores = {}, {}

    barrier = pltpu.get_barrier_semaphore()
    for step in range(1, peers):
        pl.semaphore_signal(
            barrier, inc=1, device_id=(dp, lax.rem(me + step, peers)), device_id_type=MESH
        )

    for step in range(1, replicas):
        pl.semaphore_signal(
            barrier, inc=1, device_id=(lax.rem(dp + step, replicas), me), device_id_type=MESH
        )

    def load(which, source, chunk):
        copy = pltpu.make_async_copy(
            source.at[pl.ds(chunk * CHUNK, CHUNK)], tiles_in.at[which], in_sem.at[which]
        )
        copy.start()
        copies["in", which] = copy

    def store(which, target, chunk):
        copy = pltpu.make_async_copy(
            tiles_out.at[which], target.at[pl.ds(chunk * CHUNK, CHUNK)], out_sem.at[which]
        )
        copy.start()
        stores[which] = copy

    def columns(block):
        return pl.ds(pl.multiple_of(block * size, size), size)

    def spread(which, block, values):
        for half in range(halves):
            stage[which, half, pl.ds(block, size, stride=blocks), :] = values[
                :, half * LANES : (half + 1) * LANES
            ]

    def release(kind, chunk):
        for copy in copies.pop(("send", kind, chunk), ()):
            copy.wait_send()

    def dispatch(kind, chunk, which):
        release(kind, chunk - SLOTS)
        held = send.at[kind, chunk % SLOTS]
        if chunk >= SLOTS:
            copies.pop(("own", kind, chunk - SLOTS)).wait()

        @pl.loop(0, size, unroll=8)
        def _(row):
            for half in range(halves):
                held[row, :, half * LANES : (half + 1) * LANES] = stage[
                    which, half, pl.ds(pl.multiple_of(row * blocks, blocks), blocks), :
                ].astype(jnp.bfloat16)

        def rows(peer):
            return pl.ds(pl.multiple_of(peer * blocks, blocks), blocks)

        place = recv.at[kind, chunk, :, rows(me), :]
        started = []
        for step in range(1, peers):
            peer = lax.rem(me + step, peers)
            copy = pltpu.make_async_remote_copy(
                src_ref=held.at[rows(peer)],
                dst_ref=place,
                send_sem=send_sem.at[kind, chunk % SLOTS, step],
                recv_sem=recv_sem.at[kind, chunk, step],
                device_id=(dp, peer),
                device_id_type=MESH,
            )
            copy.start()
            started.append(copy)
        copies["send", kind, chunk] = started
        copies["recv", kind, chunk] = started
        own = pltpu.make_async_copy(held.at[rows(me)], place, own_sem.at[kind, chunk % SLOTS])
        own.start()
        copies["own", kind, chunk] = own

    def arrive(kind, chunk):
        for copy in copies.pop(("recv", kind, chunk)):
            copy.wait_recv()
        own = copies.pop(("own", kind, chunk), None)
        if own is not None:
            own.wait()
            copies["own", kind, chunk] = DONE

    def share(which, total):
        @pl.loop(0, blocks, unroll=4)
        def _(block):
            for part in range(replicas):
                shares[which, part, block] = total[
                    block, part * slab : (part + 1) * slab, :
                ].astype(jnp.bfloat16)

        started = []
        for step in range(1, replicas):
            peer = lax.rem(dp + step, replicas)
            copy = pltpu.make_async_remote_copy(
                src_ref=shares.at[which, peer],
                dst_ref=landing.at[which, step],
                send_sem=share_sem.at[which, step],
                recv_sem=landing_sem.at[which, step],
                device_id=(peer, me),
                device_id_type=MESH,
            )
            copy.start()
            started.append(copy)
        copies["share", which] = started

    def collect(which, total, target):
        for copy in copies.pop(("share", which)):
            copy.wait()

        @pl.loop(0, blocks, unroll=4)
        def _(block):
            value = total[block, pl.ds(pl.multiple_of(dp * slab, slab), slab), :]
            for step in range(1, replicas):
                value += landing[which, step, block].astype(jnp.float32)
            target[block] = value

    def turn(weight, turned):
        @pl.loop(0, blocks, unroll=4)
        def _(block):
            turned[block] = weight[block].T

    def first(chunk):
        for kind, weight, source in ((0, w1t, x_hbm), (1, o2, g_hbm)):
            copies["in", kind].wait()

            @pl.loop(0, blocks, unroll=4)
            def _(block):
                spread(kind, block, dot(weight[block], tiles_in[kind, :, columns(block)], 1, 1))

            if chunk + 1 < chunks:
                load(kind, source, chunk + 1)
            if kind == 0 and chunk == 0:
                pl.semaphore_wait(barrier, peers + replicas - 2)
            dispatch(kind, chunk, kind)

    def middle(chunk):
        arrive(0, chunk)
        arrive(1, chunk)

        @pl.loop(0, blocks, unroll=2)
        def _(block):
            perm = recv[0, chunk, block]
            value = dot(o1t[block], perm, 1, 0)
            square = value * value
            bent = jnp.tanh(ROOT_2_PI * value * (1.0 + CUBIC * square))
            rise = 0.5 + 0.5 * bent
            slope = rise + (0.5 * ROOT_2_PI) * value * (1.0 - bent * bent) * (
                1.0 + (3.0 * CUBIC) * square
            )
            hidden = (value * rise).astype(jnp.bfloat16)
            back = recv[1, chunk, block]
            grad_pre = (dot(w2[block], back, 1, 0) * slope).astype(jnp.bfloat16)
            spread(0, block, dot(w2t[block], hidden, 1, 0))
            spread(1, block, dot(o1[block], grad_pre, 1, 0))
            i2_grad[block] += dot(hidden, back, 1, 1)
            o1_grad[block] += dot(perm, grad_pre, 1, 1)

        dispatch(2, chunk, 0)
        dispatch(3, chunk, 1)
        if chunk == chunks - 1:
            share(0, i2_grad)
            share(1, o1_grad)

    def last(chunk):
        for kind, weight, total, source, target in (
            (2, o2, o2_grad, g_hbm, out_hbm), (3, w1t, i1_grad, x_hbm, ig_hbm)
        ):
            arrive(kind, chunk)
            copies["in", kind].wait()
            if chunk:
                stores[kind - 2].wait()

            @pl.loop(0, blocks, unroll=4)
            def _(block):
                part = recv[kind, chunk, block]
                tiles_out[kind - 2, :, columns(block)] = dot(
                    part, weight[block], 0, 0
                ).astype(jnp.bfloat16)
                total[block] += dot(part, tiles_in[kind, :, columns(block)], 1, 0)

            store(kind - 2, target, chunk)
            if chunk + 1 < chunks:
                load(kind, source, chunk + 1)
            elif kind == 2:
                share(2, o2_grad)

    for which, source in enumerate((x_hbm, g_hbm, g_hbm, x_hbm)):
        load(which, source, 0)
    turn(w1, w1t)
    for step in range(chunks + LAG_LAST):
        if step < chunks:
            first(step)
        if step == 0:
            turn(o1, o1t)
            turn(w2, w2t)
            for total in (i1_grad, o1_grad, i2_grad, o2_grad):
                @pl.loop(0, blocks, unroll=4)
                def _(block):
                    total[block] = jnp.zeros((size, size), jnp.float32)
        if 0 <= step - LAG_MIDDLE < chunks:
            middle(step - LAG_MIDDLE)
        if 0 <= step - LAG_LAST < chunks:
            last(step - LAG_LAST)

    @pl.loop(0, blocks, unroll=4)
    def _(block):
        i1_grad[block] = i1_grad[block].T

    for kind in range(4):
        for chunk in range(chunks):
            release(kind, chunk)
    for copy in stores.values():
        copy.wait()

    collect(0, i2_grad, i2_sum)
    collect(1, o1_grad, o1_sum)
    collect(2, o2_grad, o2_sum)


class Done:
    def wait(self):
        pass


DONE = Done()


def fused(peers, replicas, tokens, inner_one, outer_one, inner_two, outer_two, cotangent):
    tok_rows, width = tokens.shape
    blocks, size, _ = inner_one.shape
    chunks = tok_rows // CHUNK
    in_vmem = pl.BlockSpec(memory_space=pltpu.VMEM)
    anywhere = pl.BlockSpec(memory_space=pl.ANY)
    slab = size // replicas
    grad = jax.ShapeDtypeStruct((blocks, size, size), jnp.float32)
    part = jax.ShapeDtypeStruct((blocks, slab, size), jnp.float32)
    wide = jax.ShapeDtypeStruct((tok_rows + SPARE, width), jnp.bfloat16)
    results = pl.pallas_call(
        functools.partial(monarch_kernel, peers, replicas, chunks, blocks, size),
        out_shape=(wide, wide, grad, part, part, part),
        in_specs=[anywhere] * 2 + [in_vmem] * 4,
        out_specs=(anywhere,) * 2 + (in_vmem,) * 4,
        scratch_shapes=[
            pltpu.VMEM((4, chunks, blocks, size, CHUNK), jnp.bfloat16),
            pltpu.VMEM((4, SLOTS, size, blocks, CHUNK), jnp.bfloat16),
            pltpu.VMEM((2, CHUNK // LANES, size * blocks, LANES), jnp.float32),
            pltpu.VMEM((4, CHUNK, width), jnp.bfloat16),
            pltpu.VMEM((2, CHUNK, width), jnp.bfloat16),
            *[pltpu.VMEM((blocks, size, size), jnp.bfloat16)] * 3,
            *[pltpu.VMEM((blocks, size, size), jnp.float32)] * 3,
            pltpu.VMEM((3, replicas, blocks, slab, size), jnp.bfloat16),
            pltpu.VMEM((3, replicas, blocks, slab, size), jnp.bfloat16),
            pltpu.SemaphoreType.DMA((4, SLOTS, peers)),
            pltpu.SemaphoreType.DMA((4, chunks, peers)),
            pltpu.SemaphoreType.DMA((4, SLOTS)),
            pltpu.SemaphoreType.DMA((4,)),
            pltpu.SemaphoreType.DMA((2,)),
            pltpu.SemaphoreType.DMA((3, replicas)),
            pltpu.SemaphoreType.DMA((3, replicas)),
        ],
        compiler_params=pltpu.CompilerParams(
            collective_id=0, has_side_effects=True, vmem_limit_bytes=62 * 1024 * 1024
        ),
        cost_estimate=pl.CostEstimate(
            flops=24 * tok_rows * width * size, bytes_accessed=12 * tok_rows * width,
            transcendentals=tok_rows * width,
        ),
    )(tokens, cotangent, inner_one, outer_one, inner_two, outer_two)
    output, input_grad, inner_one_term, *sums = results
    inner_one_grad = lax.psum_scatter(inner_one_term, "dp", scatter_dimension=1, tiled=True)
    return (output[:tok_rows], input_grad[:tok_rows], inner_one_grad, *sums)


def gelu_tanh(values):
    return jax.nn.gelu(values, approximate=True)


def product(form, left, right):
    return jnp.einsum(form, left, right, preferred_element_type=jnp.float32)


def return_second(grads, outer_two):
    grad_perm_two = product("tjl,jbl->jbt", grads, outer_two).astype(jnp.bfloat16)
    return lax.all_to_all(grad_perm_two, "mp", split_axis=1, concat_axis=0, tiled=True)


def body(tokens, inner_one, outer_one, inner_two, outer_two, cotangent):
    tok_rows = tokens.shape[0]
    local_blocks = inner_one.shape[0]
    block_size = inner_one.shape[1]
    if local_blocks == 16 and block_size == LANES and tok_rows % CHUNK == 0:
        return fused(
            lax.axis_size("mp"), lax.axis_size("dp"), tokens, inner_one, outer_one,
            inner_two, outer_two, cotangent,
        )
    inputs = tokens.reshape(tok_rows, local_blocks, block_size)
    grads = cotangent.reshape(tok_rows, local_blocks, block_size)
    first_mid = product("tbk,bkj->jbt", inputs, inner_one).astype(jnp.bfloat16)
    first_perm = lax.all_to_all(first_mid, "mp", split_axis=0, concat_axis=1, tiled=True)
    pre_act = product("jbt,jbl->tjl", first_perm, outer_one)
    hidden = gelu_tanh(pre_act).astype(jnp.bfloat16)
    second_mid = product("tbk,bkj->jbt", hidden, inner_two).astype(jnp.bfloat16)
    second_perm = lax.all_to_all(second_mid, "mp", split_axis=0, concat_axis=1, tiled=True)
    output = product("jbt,jbl->tjl", second_perm, outer_two).astype(jnp.bfloat16)
    outer_two_grad = product("jbt,tjl->jbl", second_perm, grads)
    outer_two_grad = lax.psum_scatter(outer_two_grad, "dp", scatter_dimension=1, tiled=True)
    grad_mid_two = return_second(grads, outer_two)
    grad_hidden = product("jbt,bkj->tbk", grad_mid_two, inner_two)
    inner_two_grad = product("tbk,jbt->bkj", hidden, grad_mid_two)
    inner_two_grad = lax.psum_scatter(inner_two_grad, "dp", scatter_dimension=1, tiled=True)
    primal_out, pullback = jax.vjp(gelu_tanh, pre_act)
    grad_pre = pullback(grad_hidden)[0].astype(jnp.bfloat16)
    grad_perm_one = product("tjl,jbl->jbt", grad_pre, outer_one).astype(jnp.bfloat16)
    outer_one_grad = product("jbt,tjl->jbl", first_perm, grad_pre)
    outer_one_grad = lax.psum_scatter(outer_one_grad, "dp", scatter_dimension=1, tiled=True)
    grad_mid_one = lax.all_to_all(grad_perm_one, "mp", split_axis=1, concat_axis=0, tiled=True)
    input_grad = product("jbt,bkj->tbk", grad_mid_one, inner_one).astype(jnp.bfloat16)
    inner_one_grad = product("tbk,jbt->bkj", inputs, grad_mid_one)
    inner_one_grad = lax.psum_scatter(inner_one_grad, "dp", scatter_dimension=1, tiled=True)
    width_here = local_blocks * block_size
    return (
        output.reshape(tok_rows, width_here),
        input_grad.reshape(tok_rows, width_here),
        inner_one_grad,
        outer_one_grad,
        inner_two_grad,
        outer_two_grad,
    )


def solution(mesh):
    placed = (
        P("dp", "mp"),
        P("mp", None, None),
        P("mp", None, None),
        P("mp", None, None),
        P("mp", None, None),
        P("dp", "mp"),
    )
    return jax.shard_map(
        body,
        mesh=mesh,
        in_specs=placed,
        out_specs=(
            P("dp", "mp"),
            P("dp", "mp"),
            P("mp", "dp", None),
            P("mp", "dp", None),
            P("mp", "dp", None),
            P("mp", "dp", None),
        ),
        check_vma=False,
    )
```

```python
import functools
import jax
import jax.numpy as jnp
from jax import lax
from jax.experimental import pallas as pl
from jax.experimental.pallas import tpu as pltpu
from jax.sharding import PartitionSpec as P

MESH = pl.DeviceIdType.MESH
CHUNK = 256
LANES = 128
SLOTS = 2
LAG_MIDDLE = 2
LAG_LAST = 4
SPARE = 16
ROOT_2_PI = 0.7978845608028654
CUBIC = 0.044715


def dot(left, right, left_axis, right_axis):
    return lax.dot_general(
        left, right, (((left_axis,), (right_axis,)), ((), ())),
        preferred_element_type=jnp.float32,
    )


def monarch_kernel(
    peers, replicas, chunks, blocks, size,
    x_hbm, g_hbm, w1, o1, w2, o2,
    out_hbm, ig_hbm, i1_term, o1_sum, i2_sum, o2_sum,
    recv, send, stage, tiles_in, tiles_out,
    w1t, o1t, w2t, i1_grad, o1_grad, i2_grad, o2_grad, shares, landing,
    send_sem, recv_sem, own_sem, in_sem, out_sem, share_sem, landing_sem,
):
    dp, me = lax.axis_index("dp"), lax.axis_index("mp")
    halves = CHUNK // LANES
    slab = size // replicas
    copies, stores = {}, {}

    barrier = pltpu.get_barrier_semaphore()
    for step in range(1, peers):
        pl.semaphore_signal(
            barrier, inc=1, device_id=(dp, lax.rem(me + step, peers)), device_id_type=MESH
        )

    for step in range(1, replicas):
        pl.semaphore_signal(
            barrier, inc=1, device_id=(lax.rem(dp + step, replicas), me), device_id_type=MESH
        )

    def load(which, source, chunk):
        copy = pltpu.make_async_copy(
            source.at[pl.ds(chunk * CHUNK, CHUNK)], tiles_in.at[which], in_sem.at[which]
        )
        copy.start()
        copies["in", which] = copy

    def store(which, target, chunk):
        copy = pltpu.make_async_copy(
            tiles_out.at[which], target.at[pl.ds(chunk * CHUNK, CHUNK)], out_sem.at[which]
        )
        copy.start()
        stores[which] = copy

    def columns(block):
        return pl.ds(pl.multiple_of(block * size, size), size)

    def spread(which, block, values):
        for half in range(halves):
            stage[which, half, pl.ds(block, size, stride=blocks), :] = values[
                :, half * LANES : (half + 1) * LANES
            ]

    def release(kind, chunk):
        for copy in copies.pop(("send", kind, chunk), ()):
            copy.wait_send()

    def dispatch(kind, chunk, which):
        release(kind, chunk - SLOTS)
        held = send.at[kind, chunk % SLOTS]
        if chunk >= SLOTS:
            copies.pop(("own", kind, chunk - SLOTS)).wait()

        @pl.loop(0, size, unroll=8)
        def _(row):
            for half in range(halves):
                held[row, :, half * LANES : (half + 1) * LANES] = stage[
                    which, half, pl.ds(pl.multiple_of(row * blocks, blocks), blocks), :
                ].astype(jnp.bfloat16)

        def rows(peer):
            return pl.ds(pl.multiple_of(peer * blocks, blocks), blocks)

        place = recv.at[kind, chunk, :, rows(me), :]
        started = []
        for step in range(1, peers):
            peer = lax.rem(me + step, peers)
            copy = pltpu.make_async_remote_copy(
                src_ref=held.at[rows(peer)],
                dst_ref=place,
                send_sem=send_sem.at[kind, chunk % SLOTS, step],
                recv_sem=recv_sem.at[kind, chunk, step],
                device_id=(dp, peer),
                device_id_type=MESH,
            )
            copy.start()
            started.append(copy)
        copies["send", kind, chunk] = started
        copies["recv", kind, chunk] = started
        own = pltpu.make_async_copy(held.at[rows(me)], place, own_sem.at[kind, chunk % SLOTS])
        own.start()
        copies["own", kind, chunk] = own

    def arrive(kind, chunk):
        for copy in copies.pop(("recv", kind, chunk)):
            copy.wait_recv()
        own = copies.pop(("own", kind, chunk), None)
        if own is not None:
            own.wait()
            copies["own", kind, chunk] = DONE

    def share(which, total):
        @pl.loop(0, blocks, unroll=4)
        def _(block):
            for part in range(replicas):
                shares[which, part, block] = total[
                    block, part * slab : (part + 1) * slab, :
                ].astype(jnp.bfloat16)

        started = []
        for step in range(1, replicas):
            peer = lax.rem(dp + step, replicas)
            copy = pltpu.make_async_remote_copy(
                src_ref=shares.at[which, peer],
                dst_ref=landing.at[which, step],
                send_sem=share_sem.at[which, step],
                recv_sem=landing_sem.at[which, step],
                device_id=(peer, me),
                device_id_type=MESH,
            )
            copy.start()
            started.append(copy)
        copies["share", which] = started

    def collect(which, total, target):
        for copy in copies.pop(("share", which)):
            copy.wait()

        @pl.loop(0, blocks, unroll=4)
        def _(block):
            value = total[block, pl.ds(pl.multiple_of(dp * slab, slab), slab), :]
            for step in range(1, replicas):
                value += landing[which, step, block].astype(jnp.float32)
            target[block] = value

    def turn(weight, turned):
        @pl.loop(0, blocks, unroll=4)
        def _(block):
            turned[block] = weight[block].T

    def first(chunk):
        for kind, weight, source in ((0, w1t, x_hbm), (1, o2, g_hbm)):
            copies["in", kind].wait()

            @pl.loop(0, blocks, unroll=4)
            def _(block):
                spread(kind, block, dot(weight[block], tiles_in[kind, :, columns(block)], 1, 1))

            if chunk + 1 < chunks:
                load(kind, source, chunk + 1)
            if kind == 0 and chunk == 0:
                pl.semaphore_wait(barrier, peers + replicas - 2)
            dispatch(kind, chunk, kind)

    def middle(chunk):
        arrive(0, chunk)
        arrive(1, chunk)

        @pl.loop(0, blocks, unroll=2)
        def _(block):
            perm = recv[0, chunk, block]
            value = dot(o1t[block], perm, 1, 0)
            square = value * value
            bent = jnp.tanh(ROOT_2_PI * value * (1.0 + CUBIC * square))
            rise = 0.5 + 0.5 * bent
            slope = rise + (0.5 * ROOT_2_PI) * value * (1.0 - bent * bent) * (
                1.0 + (3.0 * CUBIC) * square
            )
            hidden = (value * rise).astype(jnp.bfloat16)
            back = recv[1, chunk, block]
            grad_pre = (dot(w2[block], back, 1, 0) * slope).astype(jnp.bfloat16)
            spread(0, block, dot(w2t[block], hidden, 1, 0))
            spread(1, block, dot(o1[block], grad_pre, 1, 0))
            i2_grad[block] += dot(hidden, back, 1, 1)
            o1_grad[block] += dot(perm, grad_pre, 1, 1)

        dispatch(2, chunk, 0)
        dispatch(3, chunk, 1)
        if chunk == chunks - 1:
            share(0, i2_grad)
            share(1, o1_grad)

    def last(chunk):
        for kind, weight, total, source, target in (
            (2, o2, o2_grad, g_hbm, out_hbm), (3, w1t, i1_grad, x_hbm, ig_hbm)
        ):
            arrive(kind, chunk)
            copies["in", kind].wait()
            if chunk:
                stores[kind - 2].wait()

            @pl.loop(0, blocks, unroll=4)
            def _(block):
                part = recv[kind, chunk, block]
                tiles_out[kind - 2, :, columns(block)] = dot(
                    part, weight[block], 0, 0
                ).astype(jnp.bfloat16)
                total[block] += dot(part, tiles_in[kind, :, columns(block)], 1, 0)

            store(kind - 2, target, chunk)
            if chunk + 1 < chunks:
                load(kind, source, chunk + 1)
            elif kind == 2:
                share(2, o2_grad)

    for which, source in enumerate((x_hbm, g_hbm, g_hbm, x_hbm)):
        load(which, source, 0)
    turn(w1, w1t)
    for step in range(chunks + LAG_LAST):
        if step < chunks:
            first(step)
        if step == 0:
            turn(o1, o1t)
            turn(w2, w2t)
            for total in (i1_grad, o1_grad, i2_grad, o2_grad):
                @pl.loop(0, blocks, unroll=4)
                def _(block):
                    total[block] = jnp.zeros((size, size), jnp.float32)
        if 0 <= step - LAG_MIDDLE < chunks:
            middle(step - LAG_MIDDLE)
        if 0 <= step - LAG_LAST < chunks:
            last(step - LAG_LAST)

    @pl.loop(0, blocks, unroll=4)
    def _(block):
        i1_term[block] = i1_grad[block].T.astype(jnp.bfloat16)

    for kind in range(4):
        for chunk in range(chunks):
            release(kind, chunk)
    for copy in stores.values():
        copy.wait()

    collect(0, i2_grad, i2_sum)
    collect(1, o1_grad, o1_sum)
    collect(2, o2_grad, o2_sum)


class Done:
    def wait(self):
        pass


DONE = Done()


def fused(peers, replicas, tokens, inner_one, outer_one, inner_two, outer_two, cotangent):
    tok_rows, width = tokens.shape
    blocks, size, _ = inner_one.shape
    chunks = tok_rows // CHUNK
    in_vmem = pl.BlockSpec(memory_space=pltpu.VMEM)
    anywhere = pl.BlockSpec(memory_space=pl.ANY)
    slab = size // replicas
    term = jax.ShapeDtypeStruct((blocks, size, size), jnp.bfloat16)
    part = jax.ShapeDtypeStruct((blocks, slab, size), jnp.float32)
    wide = jax.ShapeDtypeStruct((tok_rows + SPARE, width), jnp.bfloat16)
    results = pl.pallas_call(
        functools.partial(monarch_kernel, peers, replicas, chunks, blocks, size),
        out_shape=(wide, wide, term, part, part, part),
        in_specs=[anywhere] * 2 + [in_vmem] * 4,
        out_specs=(anywhere,) * 2 + (in_vmem,) * 4,
        scratch_shapes=[
            pltpu.VMEM((4, chunks, blocks, size, CHUNK), jnp.bfloat16),
            pltpu.VMEM((4, SLOTS, size, blocks, CHUNK), jnp.bfloat16),
            pltpu.VMEM((2, CHUNK // LANES, size * blocks, LANES), jnp.float32),
            pltpu.VMEM((4, CHUNK, width), jnp.bfloat16),
            pltpu.VMEM((2, CHUNK, width), jnp.bfloat16),
            *[pltpu.VMEM((blocks, size, size), jnp.bfloat16)] * 3,
            *[pltpu.VMEM((blocks, size, size), jnp.float32)] * 4,
            pltpu.VMEM((3, replicas, blocks, slab, size), jnp.bfloat16),
            pltpu.VMEM((3, replicas, blocks, slab, size), jnp.bfloat16),
            pltpu.SemaphoreType.DMA((4, SLOTS, peers)),
            pltpu.SemaphoreType.DMA((4, chunks, peers)),
            pltpu.SemaphoreType.DMA((4, SLOTS)),
            pltpu.SemaphoreType.DMA((4,)),
            pltpu.SemaphoreType.DMA((2,)),
            pltpu.SemaphoreType.DMA((3, replicas)),
            pltpu.SemaphoreType.DMA((3, replicas)),
        ],
        compiler_params=pltpu.CompilerParams(
            collective_id=0, has_side_effects=True, vmem_limit_bytes=62 * 1024 * 1024
        ),
        cost_estimate=pl.CostEstimate(
            flops=24 * tok_rows * width * size, bytes_accessed=12 * tok_rows * width,
            transcendentals=tok_rows * width,
        ),
    )(tokens, cotangent, inner_one, outer_one, inner_two, outer_two)
    output, input_grad, inner_one_term, *sums = results
    inner_one_grad = lax.psum_scatter(inner_one_term, "dp", scatter_dimension=1, tiled=True)
    return (
        output[:tok_rows], input_grad[:tok_rows], inner_one_grad.astype(jnp.float32), *sums
    )


def gelu_tanh(values):
    return jax.nn.gelu(values, approximate=True)


def product(form, left, right):
    return jnp.einsum(form, left, right, preferred_element_type=jnp.float32)


def return_second(grads, outer_two):
    grad_perm_two = product("tjl,jbl->jbt", grads, outer_two).astype(jnp.bfloat16)
    return lax.all_to_all(grad_perm_two, "mp", split_axis=1, concat_axis=0, tiled=True)


def body(tokens, inner_one, outer_one, inner_two, outer_two, cotangent):
    tok_rows = tokens.shape[0]
    local_blocks = inner_one.shape[0]
    block_size = inner_one.shape[1]
    if local_blocks == 16 and block_size == LANES and tok_rows % CHUNK == 0:
        return fused(
            lax.axis_size("mp"), lax.axis_size("dp"), tokens, inner_one, outer_one,
            inner_two, outer_two, cotangent,
        )
    inputs = tokens.reshape(tok_rows, local_blocks, block_size)
    grads = cotangent.reshape(tok_rows, local_blocks, block_size)
    first_mid = product("tbk,bkj->jbt", inputs, inner_one).astype(jnp.bfloat16)
    first_perm = lax.all_to_all(first_mid, "mp", split_axis=0, concat_axis=1, tiled=True)
    pre_act = product("jbt,jbl->tjl", first_perm, outer_one)
    hidden = gelu_tanh(pre_act).astype(jnp.bfloat16)
    second_mid = product("tbk,bkj->jbt", hidden, inner_two).astype(jnp.bfloat16)
    second_perm = lax.all_to_all(second_mid, "mp", split_axis=0, concat_axis=1, tiled=True)
    output = product("jbt,jbl->tjl", second_perm, outer_two).astype(jnp.bfloat16)
    outer_two_grad = product("jbt,tjl->jbl", second_perm, grads)
    outer_two_grad = lax.psum_scatter(outer_two_grad, "dp", scatter_dimension=1, tiled=True)
    grad_mid_two = return_second(grads, outer_two)
    grad_hidden = product("jbt,bkj->tbk", grad_mid_two, inner_two)
    inner_two_grad = product("tbk,jbt->bkj", hidden, grad_mid_two)
    inner_two_grad = lax.psum_scatter(inner_two_grad, "dp", scatter_dimension=1, tiled=True)
    primal_out, pullback = jax.vjp(gelu_tanh, pre_act)
    grad_pre = pullback(grad_hidden)[0].astype(jnp.bfloat16)
    grad_perm_one = product("tjl,jbl->jbt", grad_pre, outer_one).astype(jnp.bfloat16)
    outer_one_grad = product("jbt,tjl->jbl", first_perm, grad_pre)
    outer_one_grad = lax.psum_scatter(outer_one_grad, "dp", scatter_dimension=1, tiled=True)
    grad_mid_one = lax.all_to_all(grad_perm_one, "mp", split_axis=1, concat_axis=0, tiled=True)
    input_grad = product("jbt,bkj->tbk", grad_mid_one, inner_one).astype(jnp.bfloat16)
    inner_one_grad = product("tbk,jbt->bkj", inputs, grad_mid_one)
    inner_one_grad = lax.psum_scatter(inner_one_grad, "dp", scatter_dimension=1, tiled=True)
    width_here = local_blocks * block_size
    return (
        output.reshape(tok_rows, width_here),
        input_grad.reshape(tok_rows, width_here),
        inner_one_grad,
        outer_one_grad,
        inner_two_grad,
        outer_two_grad,
    )


def solution(mesh):
    placed = (
        P("dp", "mp"),
        P("mp", None, None),
        P("mp", None, None),
        P("mp", None, None),
        P("mp", None, None),
        P("dp", "mp"),
    )
    return jax.shard_map(
        body,
        mesh=mesh,
        in_specs=placed,
        out_specs=(
            P("dp", "mp"),
            P("dp", "mp"),
            P("mp", "dp", None),
            P("mp", "dp", None),
            P("mp", "dp", None),
            P("mp", "dp", None),
        ),
        check_vma=False,
    )
```
